768 devices in a mesh: blk: 12 (over z_hi, x), group: 64 (over y, z_lo, core).
Axes of the slice: x: 4, y: 8, z: 12 (z_hi: 3, z_lo: 4; z = z_hi * 4 + z_lo), core: 2. Of those that a mesh axis runs over, the one named last changes fastest.
Arguments:
- picture_embeds_raw: bfloat16 [196608, 1152], P(('blk', 'group')), may hold values from -0.1796875 to 0.1796875
- caption_embeds_raw: bfloat16 [196608, 1152], P(('blk', 'group')), may hold values from -0.1796875 to 0.1796875
- sharpness_factor: float32 [], replicated, may hold values from 4 to 16
- additive_shift_term: float32 [], replicated, may hold values from -4 to -1
Outputs:
- row_loss: float32 [196608], P(('blk', 'group'))
- image_grad: bfloat16 [196608, 1152], P(('blk', 'group'))
- text_grad: bfloat16 [196608, 1152], P(('blk', 'group'))
The draws below stay inside these ranges and needn't reach their ends.
All inputs are finite; a program needn't handle non-finite values.
Results may differ from the reference program's by a relative error of at most 0.009.
Values may be sent and summed in bfloat16 or wider, within the bound.
A program may use at most 64 MiB of HBM per device.

```python
import math
import jax
import jax.numpy as jnp
from jax import lax

D = 1152
TOK_DEV = 256
STEPS = 5
TOKENS = 196608
N_BLK = 12
N_GROUP = 64


def steps_of(own_key, extent, pieces, least, top_value):
    def one(position, parts):
        heights = jax.random.uniform(jax.random.fold_in(jax.random.fold_in(own_key, 6), position), (parts,), jnp.float32, least / len(pieces), top_value / len(pieces))
        return jnp.repeat(jnp.exp(heights), extent[position] // parts).reshape((-1,) + (1,) * (len(extent) - position - 1))

    level = one(*pieces[0])
    for cut in pieces[1:]:
        level = level * one(*cut)
    return level


def normal_values(stream_key, dims, scale, bound, cuts=(), kind=jnp.bfloat16):
    entries = scale * jax.random.normal(stream_key, dims, jnp.float32)
    if cuts:
        entries = entries * steps_of(stream_key, dims, cuts, -0.22, 0.18)
    return jnp.clip(entries, -bound, bound).astype(kind)


def setup_inputs(seed: int = 0) -> dict:
    streams_of = jax.random.split(jax.random.key(seed), 5)
    return {
        "picture_embeds_raw": normal_values(streams_of[0], (TOKENS, D), 0.03, 0.1796875, ((0, 768),)),
        "caption_embeds_raw": normal_values(streams_of[1], (TOKENS, D), 0.03, 0.1796875, ((0, 768),)),
        "sharpness_factor": jnp.clip(jnp.exp(jax.random.uniform(streams_of[2], (), jnp.float32, math.log(4.0), math.log(16.0))), 4.0, 16.0),
        "additive_shift_term": jnp.clip(jax.random.uniform(streams_of[3], (), jnp.float32, -4.0, -1.0), -4.0, -1.0),
    }


def normalize(raw):
    rawf = raw.astype(jnp.float32)
    norms = jnp.sqrt(lax.optimization_barrier(jnp.sum(rawf * rawf, axis=-1, keepdims=True)) + 1e-06)
    return ((rawf / norms).astype(jnp.bfloat16), norms)

def unnormalize(grads, raw, norms):
    rawf = raw.astype(jnp.float32)
    inner = lax.optimization_barrier(jnp.sum(rawf * grads, axis=-1, keepdims=True))
    return ((grads - rawf * inner / (norms * norms)) / norms).astype(jnp.bfloat16)

def widened_precision_entries(value):
    return lax.optimization_barrier(value).astype(jnp.float32)

def reference(picture_embeds_raw, caption_embeds_raw, sharpness_factor, additive_shift_term):
    normalized_picture_entries, image_norms = normalize(picture_embeds_raw)
    text_unit, text_norms = normalize(caption_embeds_raw)
    picture_group_slice = widened_precision_entries(normalized_picture_entries).reshape(N_BLK, N_GROUP, TOK_DEV, D)
    texts_all = widened_precision_entries(text_unit).reshape(N_BLK, N_GROUP, TOK_DEV, D)
    diagonal = jnp.eye(TOK_DEV, dtype=bool)

    def score(caption_group_slice, with_labels):
        couple_similarity = jnp.einsum('moqy,mosy->moqs', picture_group_slice, caption_group_slice) * sharpness_factor + additive_shift_term
        desired_polarity = jnp.where(diagonal, 1.0, -1.0).astype(jnp.float32) if with_labels else jnp.float32(-1.0)
        losses = lax.optimization_barrier(jnp.sum(jax.nn.softplus(-desired_polarity * couple_similarity), axis=-1))
        couple_weight_factor = widened_precision_entries((-desired_polarity * jax.nn.sigmoid(-desired_polarity * couple_similarity) * sharpness_factor).astype(jnp.bfloat16))
        return (losses, jnp.einsum('bgij,bgjd->bgid', couple_weight_factor, caption_group_slice), jnp.einsum('bgij,bgid->bgjd', couple_weight_factor, picture_group_slice))
    row_loss = jnp.zeros((N_BLK, N_GROUP, TOK_DEV), jnp.float32)
    image_sum = jnp.zeros((N_BLK, N_GROUP, TOK_DEV, D), jnp.float32)
    text_sum = jnp.zeros((N_BLK, N_GROUP, TOK_DEV, D), jnp.float32)
    for offset in range(STEPS):
        losses, image_part, text_part = score(jnp.roll(texts_all, offset, axis=0), offset == 0)
        row_loss = row_loss + losses
        image_sum = image_sum + image_part
        text_sum = text_sum + jnp.roll(text_part, -offset, axis=0)
    losses, image_part, text_part = score(jnp.roll(texts_all, 1, axis=1), False)
    row_loss = row_loss + losses
    image_sum = image_sum + image_part
    text_sum = text_sum + jnp.roll(text_part, -1, axis=1)
    image_grad = unnormalize(image_sum.reshape(TOKENS, D), picture_embeds_raw, image_norms)
    text_grad = unnormalize(text_sum.reshape(TOKENS, D), caption_embeds_raw, text_norms)
    return (row_loss.reshape(TOKENS), image_grad, text_grad)
```

```python
import functools
import jax
import jax.numpy as jnp
from jax import lax
from jax.experimental import pallas as pl
from jax.experimental.pallas import tpu as pltpu
from jax.sharding import PartitionSpec as P

MESH = pl.DeviceIdType.MESH
NX = 4
CHUNKS = 8
IMAGE, TEXT = 0, 1


def partners():
    blk, group = lax.axis_index("blk"), lax.axis_index("group")
    n_blk, n_group = lax.axis_size("blk"), lax.axis_size("group")
    x = lax.rem(blk, NX)
    plane = blk - x
    return dict(
        x=x,
        ahead=(lax.rem(blk + NX, n_blk), group),
        behind=(lax.rem(blk + n_blk - NX, n_blk), group),
        along=[None] + [(plane + lax.rem(x + d, NX), group) for d in range(1, NX)],
        after=(blk, lax.rem(group + 1, n_group)),
        before=(blk, lax.rem(group + n_group - 1, n_group)),
    )


def kernel(
    scal, pic, cap, loss_out, image_out, text_out,
    raw, unit, inv, block, near, acc, loss_acc,
    in_sem, out_sem, z_send, z_recv, x_send, x_recv, g_send, g_recv,
):
    rows, width = unit.shape[1], unit.shape[2]
    part = rows // CHUNKS
    sharp, shift = scal[0], scal[1]
    who = partners()
    x = who["x"]

    loads = [
        pltpu.make_async_copy(src, raw.at[side], in_sem.at[side])
        for side, src in ((IMAGE, pic), (TEXT, cap))
    ]
    for load in loads:
        load.start()

    barrier = pltpu.get_barrier_semaphore()
    others = [who["ahead"], who["behind"], who["after"], who["before"]] + who["along"][1:]
    for other in others:
        pl.semaphore_signal(barrier, inc=1, device_id=other, device_id_type=MESH)

    def z_copy(side, k):
        return pltpu.make_async_remote_copy(
            src_ref=unit.at[side, pl.ds(k * part, part)],
            dst_ref=block.at[side, k, 0],
            send_sem=z_send.at[side, k],
            recv_sem=z_recv.at[side, k],
            device_id=who["ahead"] if side == TEXT else who["behind"],
            device_id_type=MESH,
        )

    def x_copy(side, d, k, late):
        own = unit.at[side, pl.ds(k * part, part)]
        return pltpu.make_async_remote_copy(
            src_ref=block.at[side, k, 0] if late else own,
            dst_ref=block.at[side, k, d],
            send_sem=x_send.at[side, d - 1, k],
            recv_sem=x_recv.at[side, d - 1, k],
            device_id=who["along"][d],
            device_id_type=MESH,
        )

    def g_copy(side, k):
        return pltpu.make_async_remote_copy(
            src_ref=unit.at[side, pl.ds(k * part, part)],
            dst_ref=near.at[side, pl.ds(k * part, part)],
            send_sem=g_send.at[side, k],
            recv_sem=g_recv.at[side, k],
            device_id=who["after"] if side == TEXT else who["before"],
            device_id_type=MESH,
        )

    for side in (IMAGE, TEXT):
        loads[side].wait()

        @pl.loop(0, CHUNKS)
        def _(k):
            at = pl.ds(k * part, part)
            rawf = raw[side, at].astype(jnp.float32)
            scale = 1.0 / jnp.sqrt(jnp.sum(rawf * rawf, axis=-1, keepdims=True) + 1e-06)
            inv[side, at] = scale
            unit[side, at] = (rawf * scale).astype(jnp.bfloat16)

    pl.semaphore_wait(barrier, len(others))

    @pl.loop(0, CHUNKS)
    def _(k):
        for side in (IMAGE, TEXT):
            z_copy(side, k).start()

    @pl.loop(0, CHUNKS)
    def _(k):
        for d in range(1, NX):

            @pl.when(x + d < NX)
            def _():
                x_copy(TEXT, d, k, False).start()

            @pl.when(x + d >= NX)
            def _():
                x_copy(IMAGE, d, k, False).start()

    def logits(mine, theirs):
        dots = lax.dot_general(
            mine, theirs, (((1,), (1,)), ((), ())), preferred_element_type=jnp.float32
        )
        return dots * sharp + shift

    def soft(v):
        small = jnp.exp(-jnp.abs(v))
        plus = jnp.maximum(v, 0.0) + jnp.log1p(small)
        return plus, jnp.where(v >= 0.0, 1.0, small) / (1.0 + small)

    lanes = loss_acc.shape[1]
    same = lax.broadcasted_iota(jnp.int32, (rows, rows), 0) == lax.broadcasted_iota(
        jnp.int32, (rows, rows), 1
    )
    label = jnp.where(same, 1.0, -1.0)
    plus, sig = soft(-label * logits(unit[IMAGE], unit[TEXT]))
    loss_acc[...] = sum(plus[:, i : i + lanes] for i in range(0, rows, lanes))
    coef = (-label * sig * sharp).astype(jnp.bfloat16)
    acc[IMAGE] = jnp.dot(coef, unit[TEXT], preferred_element_type=jnp.float32)
    acc[TEXT] = lax.dot_general(
        coef, unit[IMAGE], (((0,), (0,)), ((), ())), preferred_element_type=jnp.float32
    )

    def score_texts(theirs):
        plus, sig = soft(logits(unit[IMAGE], theirs))
        loss_acc[...] += plus
        coef = (sig * sharp).astype(jnp.bfloat16)
        acc[IMAGE] += jnp.dot(coef, theirs, preferred_element_type=jnp.float32)

    def score_images(theirs):
        sig = 1.0 / (1.0 + jnp.exp(-logits(unit[TEXT], theirs)))
        coef = (sig * sharp).astype(jnp.bfloat16)
        acc[TEXT] += jnp.dot(coef, theirs, preferred_element_type=jnp.float32)

    def finish_round(k):
        for side, score in ((TEXT, score_texts), (IMAGE, score_images)):
            for d in range(1, NX):
                x_copy(side, d, k, False).wait_recv()
            score(block[side, k].reshape(NX * part, width))

    @pl.loop(0, CHUNKS)
    def _(k):
        for side in (IMAGE, TEXT):
            z_copy(side, k).wait_recv()
        for d in range(1, NX):

            @pl.when(x + d >= NX)
            def _():
                x_copy(TEXT, d, k, True).start()

            @pl.when(x + d < NX)
            def _():
                x_copy(IMAGE, d, k, True).start()

        for side in (IMAGE, TEXT):
            g_copy(side, k).start()

        @pl.when(k > 0)
        def _():
            finish_round(k - 1)

    finish_round(CHUNKS - 1)

    per = NX * part
    for side, score in ((TEXT, score_texts), (IMAGE, score_images)):
        for p in range(rows // per):
            for k in range(p * NX, (p + 1) * NX):
                g_copy(side, k).wait_recv()
            score(near[side, p * per : (p + 1) * per])

    loss_out[...] = jnp.sum(loss_acc[...].T, axis=0, keepdims=True)

    def out_copy(side, k):
        at = pl.ds(k * part, part)
        out = image_out if side == IMAGE else text_out
        return pltpu.make_async_copy(raw.at[side, at], out.at[at], out_sem.at[side, k])

    for side in (IMAGE, TEXT):

        @pl.loop(0, CHUNKS)
        def _(k):
            at = pl.ds(k * part, part)
            rawf = raw[side, at].astype(jnp.float32)
            grads = acc[side, at]
            scale = inv[side, at]
            inner = jnp.sum(rawf * grads, axis=-1, keepdims=True)
            raw[side, at] = ((grads - rawf * (inner * scale * scale)) * scale).astype(jnp.bfloat16)
            out_copy(side, k).start()

    @pl.loop(0, CHUNKS)
    def _(k):
        for side in (IMAGE, TEXT):
            z_copy(side, k).wait_send()
            g_copy(side, k).wait_send()
            for d in range(1, NX):
                x_copy(side, d, k, False).wait_send()
            out_copy(side, k).wait()


def on_device(picture_embeds_raw, caption_embeds_raw, sharpness_factor, additive_shift_term):
    rows, width = picture_embeds_raw.shape
    part = rows // CHUNKS
    kind = picture_embeds_raw.dtype
    vmem, any_ = pl.BlockSpec(memory_space=pltpu.VMEM), pl.BlockSpec(memory_space=pl.ANY)
    dma = pltpu.SemaphoreType.DMA
    scalars = jnp.stack([sharpness_factor, additive_shift_term]).astype(jnp.float32)
    loss, image_grad, text_grad = pl.pallas_call(
        kernel,
        out_shape=(
            jax.ShapeDtypeStruct((1, rows), jnp.float32),
            jax.ShapeDtypeStruct((rows, width), kind),
            jax.ShapeDtypeStruct((rows, width), kind),
        ),
        in_specs=[pl.BlockSpec(memory_space=pltpu.SMEM), any_, any_],
        out_specs=(vmem, any_, any_),
        scratch_shapes=[
            pltpu.VMEM((2, rows, width), kind),
            pltpu.VMEM((2, rows, width), jnp.bfloat16),
            pltpu.VMEM((2, rows, 1), jnp.float32),
            pltpu.VMEM((2, CHUNKS, NX, part, width), jnp.bfloat16),
            pltpu.VMEM((2, rows, width), jnp.bfloat16),
            pltpu.VMEM((2, rows, width), jnp.float32),
            pltpu.VMEM((rows, NX * part), jnp.float32),
            dma((2,)),
            dma((2, CHUNKS)),
            dma((2, CHUNKS)),
            dma((2, CHUNKS)),
            dma((2, NX - 1, CHUNKS)),
            dma((2, NX - 1, CHUNKS)),
            dma((2, CHUNKS)),
            dma((2, CHUNKS)),
        ],
        compiler_params=pltpu.CompilerParams(
            collective_id=0, has_side_effects=True, vmem_limit_bytes=40 << 20
        ),
        name="paired_blocks",
    )(scalars, picture_embeds_raw, caption_embeds_raw)
    return loss.reshape(rows), image_grad, text_grad


def solution(mesh):
    in_specs = (P(("blk", "group"), None), P(("blk", "group"), None), P(), P())
    out_specs = (P(("blk", "group")), P(("blk", "group"), None), P(("blk", "group"), None))
    return jax.shard_map(
        on_device, mesh=mesh, in_specs=in_specs, out_specs=out_specs, check_vma=False
    )
```

```python
import functools
import jax
import jax.numpy as jnp
from jax import lax
from jax.experimental import pallas as pl
from jax.experimental.pallas import tpu as pltpu
from jax.sharding import PartitionSpec as P

MESH = pl.DeviceIdType.MESH
NX = 4
CHUNKS = 8
WINDOW = 3
G_LAG = 0
IMAGE, TEXT = 0, 1


def partners():
    blk, group = lax.axis_index("blk"), lax.axis_index("group")
    n_blk, n_group = lax.axis_size("blk"), lax.axis_size("group")
    x = lax.rem(blk, NX)
    plane = blk - x
    return dict(
        x=x,
        ahead=(lax.rem(blk + NX, n_blk), group),
        behind=(lax.rem(blk + n_blk - NX, n_blk), group),
        along=[None] + [(plane + lax.rem(x + d, NX), group) for d in range(1, NX)],
        after=(blk, lax.rem(group + 1, n_group)),
        before=(blk, lax.rem(group + n_group - 1, n_group)),
    )


def exchange(
    scal, pic, cap,
    image_acc, text_acc, image_raw, text_raw, loss_out,
    unit, block, loss_acc,
    in_sem, z_send, z_recv, x_send, x_recv, g_send, g_recv,
):
    rows, width = unit.shape[1], unit.shape[2]
    part = rows // CHUNKS
    half = rows // 2
    per = NX * part
    g_at = CHUNKS * per
    sharp, shift = scal[0], scal[1]
    who = partners()
    x = who["x"]

    loads = [
        pltpu.make_async_copy(src, dst, in_sem.at[side])
        for side, src, dst in ((IMAGE, pic, image_raw), (TEXT, cap, text_raw))
    ]
    for load in loads:
        load.start()

    barrier = pltpu.get_barrier_semaphore()
    others = [who["ahead"], who["behind"], who["after"], who["before"]] + who["along"][1:]
    for other in others:
        pl.semaphore_signal(barrier, inc=1, device_id=other, device_id_type=MESH)

    def z_copy(side, k):
        return pltpu.make_async_remote_copy(
            src_ref=unit.at[side, pl.ds(k * part, part)],
            dst_ref=block.at[side, pl.ds(k * per, part)],
            send_sem=z_send.at[side, k],
            recv_sem=z_recv.at[side, k],
            device_id=who["ahead"] if side == TEXT else who["behind"],
            device_id_type=MESH,
        )

    def x_copy(side, d, k, late):
        own = unit.at[side, pl.ds(k * part, part)]
        return pltpu.make_async_remote_copy(
            src_ref=block.at[side, pl.ds(k * per, part)] if late else own,
            dst_ref=block.at[side, pl.ds(k * per + d * part, part)],
            send_sem=x_send.at[side, d - 1, k],
            recv_sem=x_recv.at[side, d - 1, k],
            device_id=who["along"][d],
            device_id_type=MESH,
        )

    def g_copy(side, k):
        to = lax.rem(k * part + half, rows)
        return pltpu.make_async_remote_copy(
            src_ref=unit.at[side, pl.ds(k * part, part)],
            dst_ref=block.at[side, pl.ds(g_at + to, part)],
            send_sem=g_send.at[side, k],
            recv_sem=g_recv.at[side, k],
            device_id=who["after"] if side == TEXT else who["before"],
            device_id_type=MESH,
        )

    for side, raw in ((IMAGE, image_raw), (TEXT, text_raw)):
        loads[side].wait()

        @pl.loop(0, 2)
        def _(k):
            at = pl.ds(k * half, half)
            rawf = raw[at].astype(jnp.float32)
            scale = 1.0 / jnp.sqrt(jnp.sum(rawf * rawf, axis=-1, keepdims=True) + 1e-06)
            unit[side, at] = (rawf * scale).astype(jnp.bfloat16)

    pl.semaphore_wait(barrier, len(others))

    for k in range(WINDOW):
        for side in (IMAGE, TEXT):
            z_copy(side, k).start()

    @pl.loop(0, CHUNKS)
    def _(k):
        for d in range(1, NX):

            @pl.when(x + d < NX)
            def _():
                x_copy(TEXT, d, k, False).start()

            @pl.when(x + d >= NX)
            def _():
                x_copy(IMAGE, d, k, False).start()

    def logits(mine, theirs):
        dots = lax.dot_general(
            mine, theirs, (((1,), (1,)), ((), ())), preferred_element_type=jnp.float32
        )
        return dots * sharp + shift

    def soft(v):
        small = jnp.exp(-jnp.abs(v))
        plus = jnp.maximum(v, 0.0) + jnp.log1p(small)
        return plus, jnp.where(v >= 0.0, 1.0, small) / (1.0 + small)

    lanes = loss_acc.shape[1]

    def narrowed(plus):
        return sum(plus[:, i : i + lanes] for i in range(0, plus.shape[1], lanes))

    same = lax.broadcasted_iota(jnp.int32, (rows, rows), 0) == lax.broadcasted_iota(
        jnp.int32, (rows, rows), 1
    )
    label = jnp.where(same, 1.0, -1.0)
    plus, sig = soft(-label * logits(unit[IMAGE], unit[TEXT]))
    loss_acc[...] = narrowed(plus)
    coef = (-label * sig * sharp).astype(jnp.bfloat16)
    image_acc[...] = jnp.dot(coef, unit[TEXT], preferred_element_type=jnp.float32)
    text_acc[...] = lax.dot_general(
        coef, unit[IMAGE], (((0,), (0,)), ((), ())), preferred_element_type=jnp.float32
    )

    def score(at):
        texts, images = block[TEXT, at], block[IMAGE, at]
        plus, sig = soft(logits(unit[IMAGE], texts))
        back = 1.0 / (1.0 + jnp.exp(-logits(unit[TEXT], images)))
        loss_acc[...] += narrowed(plus)
        image_acc[...] += jnp.dot(
            (sig * sharp).astype(jnp.bfloat16), texts, preferred_element_type=jnp.float32
        )
        text_acc[...] += jnp.dot(
            (back * sharp).astype(jnp.bfloat16), images, preferred_element_type=jnp.float32
        )

    def await_round(k):
        for side in (TEXT, IMAGE):
            for d in range(1, NX):
                x_copy(side, d, k, False).wait_recv()

    def start_near(k):
        for side in (IMAGE, TEXT):
            g_copy(side, k).start()

    @pl.loop(0, CHUNKS)
    def _(k):
        for side in (IMAGE, TEXT):
            z_copy(side, k).wait_recv()
        for d in range(1, NX):

            @pl.when(x + d >= NX)
            def _():
                x_copy(TEXT, d, k, True).start()

            @pl.when(x + d < NX)
            def _():
                x_copy(IMAGE, d, k, True).start()

        @pl.when(k + WINDOW < CHUNKS)
        def _():
            for side in (IMAGE, TEXT):
                z_copy(side, k + WINDOW).start()

        @pl.when(k >= G_LAG)
        def _():
            start_near(k - G_LAG)

        @pl.when(k > 0)
        def _():
            await_round(k - 1)
            score(pl.ds((k - 1) * per, per))

    for k in range(CHUNKS - G_LAG, CHUNKS):
        start_near(k)
    for k in range(CHUNKS // 2):
        for side in (TEXT, IMAGE):
            g_copy(side, k).wait_recv()
    score(slice(g_at + half, g_at + rows))
    await_round(CHUNKS - 1)
    for k in range(CHUNKS // 2, CHUNKS):
        for side in (TEXT, IMAGE):
            g_copy(side, k).wait_recv()
    score(slice(g_at - per, g_at + half))

    loss_out[...] = jnp.sum(loss_acc[...].T, axis=0, keepdims=True)

    @pl.loop(0, CHUNKS)
    def _(k):
        for side in (IMAGE, TEXT):
            z_copy(side, k).wait_send()
            g_copy(side, k).wait_send()
            for d in range(1, NX):
                x_copy(side, d, k, False).wait_send()


def finish(
    image_acc, text_acc, image_raw, text_raw, loss, loss_out, image_out, text_out, grad, out_sem
):
    rows = image_acc.shape[0]
    loss_out[...] = loss[0]
    pieces = out_sem.shape[1]
    part = rows // pieces
    copies = []
    for side, acc, raw, out in (
        (IMAGE, image_acc, image_raw, image_out),
        (TEXT, text_acc, text_raw, text_out),
    ):
        for p in range(pieces):
            at = pl.ds(p * part, part)
            rawf = raw[at].astype(jnp.float32)
            grads = acc[at]
            scale = 1.0 / jnp.sqrt(jnp.sum(rawf * rawf, axis=-1, keepdims=True) + 1e-06)
            inner = jnp.sum(rawf * grads, axis=-1, keepdims=True)
            grad[side, at] = ((grads - rawf * (inner * scale * scale)) * scale).astype(grad.dtype)
            copies.append(
                pltpu.make_async_copy(grad.at[side, at], out.at[at], out_sem.at[side, p])
            )
            copies[-1].start()
    for copy in copies:
        copy.wait()


def on_device(picture_embeds_raw, caption_embeds_raw, sharpness_factor, additive_shift_term):
    rows, width = picture_embeds_raw.shape
    part = rows // CHUNKS
    kind = picture_embeds_raw.dtype
    vmem, any_ = pl.BlockSpec(memory_space=pltpu.VMEM), pl.BlockSpec(memory_space=pl.ANY)
    hbm = pl.BlockSpec(memory_space=pltpu.HBM)
    dma = pltpu.SemaphoreType.DMA
    scalars = jnp.stack([sharpness_factor, additive_shift_term]).astype(jnp.float32)
    sums = pl.pallas_call(
        exchange,
        out_shape=(
            pltpu.VMEM((rows, width), jnp.float32),
            pltpu.VMEM((rows, width), jnp.float32),
            pltpu.VMEM((rows, width), kind),
            pltpu.VMEM((rows, width), kind),
            pltpu.VMEM((1, rows), jnp.float32),
        ),
        in_specs=[pl.BlockSpec(memory_space=pltpu.SMEM), hbm, hbm],
        out_specs=(vmem,) * 5,
        scratch_shapes=[
            pltpu.VMEM((2, rows, width), jnp.bfloat16),
            pltpu.VMEM((2, (NX + 1) * rows, width), jnp.bfloat16),
            pltpu.VMEM((rows, min(128, NX * part)), jnp.float32),
            dma((2,)),
            dma((2, CHUNKS)),
            dma((2, CHUNKS)),
            dma((2, NX - 1, CHUNKS)),
            dma((2, NX - 1, CHUNKS)),
            dma((2, CHUNKS)),
            dma((2, CHUNKS)),
        ],
        compiler_params=pltpu.CompilerParams(
            collective_id=0, has_side_effects=True, vmem_limit_bytes=28 << 20
        ),
        name="exchange",
    )(
        scalars,
        pltpu.with_memory_space_constraint(picture_embeds_raw, pltpu.HBM),
        pltpu.with_memory_space_constraint(caption_embeds_raw, pltpu.HBM),
    )
    return pl.pallas_call(
        finish,
        out_shape=(
            jax.ShapeDtypeStruct((rows,), jnp.float32),
            jax.ShapeDtypeStruct((rows, width), kind),
            jax.ShapeDtypeStruct((rows, width), kind),
        ),
        in_specs=[vmem] * 5,
        out_specs=(vmem, any_, any_),
        scratch_shapes=[pltpu.VMEM((2, rows, width), kind), dma((2, 2))],
        compiler_params=pltpu.CompilerParams(vmem_limit_bytes=16 << 20),
        name="finish",
    )(*sums)


def solution(mesh):
    in_specs = (P(("blk", "group"), None), P(("blk", "group"), None), P(), P())
    out_specs = (P(("blk", "group")), P(("blk", "group"), None), P(("blk", "group"), None))
    return jax.shard_map(
        on_device, mesh=mesh, in_specs=in_specs, out_specs=out_specs, check_vma=False
    )
```

```python
import functools
import jax
import jax.numpy as jnp
from jax import lax
from jax.experimental import pallas as pl
from jax.experimental.pallas import tpu as pltpu
from jax.sharding import PartitionSpec as P

MESH = pl.DeviceIdType.MESH
NX = 4
CHUNKS = 8
RUN = 4
G_LEAD = 1
X_ORDER = (2, 1, 3)
IMAGE, TEXT = 0, 1


def partners():
    blk, group = lax.axis_index("blk"), lax.axis_index("group")
    n_blk, n_group = lax.axis_size("blk"), lax.axis_size("group")
    x = lax.rem(blk, NX)
    plane = blk - x
    lane = lax.rem(group // 2, RUN)
    core = lax.rem(group, 2)
    wraps = (core == 1) & (lane == RUN - 1)
    return dict(
        x=x,
        window=jnp.where(lane == 0, CHUNKS, jnp.where(wraps, 6, 4)),
        lead={
            TEXT: jnp.where(wraps, CHUNKS, G_LEAD),
            IMAGE: G_LEAD,
        },
        ahead=(lax.rem(blk + NX, n_blk), group),
        behind=(lax.rem(blk + n_blk - NX, n_blk), group),
        along=[None] + [(plane + lax.rem(x + d, NX), group) for d in range(1, NX)],
        after=(blk, lax.rem(group + 1, n_group)),
        before=(blk, lax.rem(group + n_group - 1, n_group)),
    )


def exchange(
    sharp_ref, shift_ref, pic, cap,
    image_acc, text_acc, image_raw, text_raw, loss_out,
    unit, block, loss_acc,
    in_sem, z_send, z_recv, x_send, x_recv, g_send, g_recv,
):
    rows, width = unit.shape[1], unit.shape[2]
    part = rows // CHUNKS
    half = rows // 2
    per = NX * part
    g_at = CHUNKS * per
    sharp, shift = sharp_ref[0, 0], shift_ref[0, 0]
    who = partners()
    x = who["x"]

    def load(h, side, src, dst):
        at = pl.ds(h * half, half)
        return pltpu.make_async_copy(src.at[at], dst.at[at], in_sem.at[side, h])

    inputs = ((IMAGE, pic, image_raw), (TEXT, cap, text_raw))
    for h in range(2):
        for which in inputs:
            load(h, *which).start()

    barrier = pltpu.get_barrier_semaphore()
    others = [who["ahead"], who["behind"], who["after"], who["before"]] + who["along"][1:]
    for other in others:
        pl.semaphore_signal(barrier, inc=1, device_id=other, device_id_type=MESH)

    def z_copy(side, k):
        return pltpu.make_async_remote_copy(
            src_ref=unit.at[side, pl.ds(k * part, part)],
            dst_ref=block.at[side, pl.ds(k * per, part)],
            send_sem=z_send.at[side, k],
            recv_sem=z_recv.at[side, k],
            device_id=who["ahead"] if side == TEXT else who["behind"],
            device_id_type=MESH,
        )

    def x_copy(side, d, k, late):
        own = unit.at[side, pl.ds(k * part, part)]
        return pltpu.make_async_remote_copy(
            src_ref=block.at[side, pl.ds(k * per, part)] if late else own,
            dst_ref=block.at[side, pl.ds(k * per + d * part, part)],
            send_sem=x_send.at[side, d - 1, k],
            recv_sem=x_recv.at[side, d - 1, k],
            device_id=who["along"][d],
            device_id_type=MESH,
        )

    def g_copy(side, k):
        to = lax.rem(k * part + half, rows)
        return pltpu.make_async_remote_copy(
            src_ref=unit.at[side, pl.ds(k * part, part)],
            dst_ref=block.at[side, pl.ds(g_at + to, part)],
            send_sem=g_send.at[side, k],
            recv_sem=g_recv.at[side, k],
            device_id=who["after"] if side == TEXT else who["before"],
            device_id_type=MESH,
        )

    def normalize(h):
        at = pl.ds(h * half, half)
        for side, src, raw in inputs:
            load(h, side, src, raw).wait()
            rawf = raw[at].astype(jnp.float32)
            scale = 1.0 / jnp.sqrt(jnp.sum(rawf * rawf, axis=-1, keepdims=True) + 1e-06)
            unit[side, at] = (rawf * scale).astype(jnp.bfloat16)

    normalize(0)
    pl.semaphore_wait(barrier, len(others))
    for h in range(2):
        if h == 1:
            normalize(1)
        for k in range(h * CHUNKS // 2, (h + 1) * CHUNKS // 2):
            for side in (IMAGE, TEXT):

                @pl.when(k < who["window"])
                def _():
                    z_copy(side, k).start()

                @pl.when(k < who["lead"][side])
                def _():
                    g_copy(side, k).start()

    @pl.loop(0, CHUNKS)
    def _(k):
        for d in X_ORDER:

            @pl.when(x + d < NX)
            def _():
                x_copy(TEXT, d, k, False).start()

            @pl.when(x + d >= NX)
            def _():
                x_copy(IMAGE, d, k, False).start()

    def logits(mine, theirs):
        dots = lax.dot_general(
            mine, theirs, (((1,), (1,)), ((), ())), preferred_element_type=jnp.float32
        )
        return dots * sharp + shift

    def soft(v):
        small = jnp.exp(-jnp.abs(v))
        plus = jnp.maximum(v, 0.0) + jnp.log1p(small)
        return plus, jnp.where(v >= 0.0, 1.0, small) / (1.0 + small)

    lanes = loss_acc.shape[1]

    def narrowed(plus):
        return sum(plus[:, i : i + lanes] for i in range(0, plus.shape[1], lanes))

    same = lax.broadcasted_iota(jnp.int32, (rows, rows), 0) == lax.broadcasted_iota(
        jnp.int32, (rows, rows), 1
    )
    label = jnp.where(same, 1.0, -1.0)
    plus, sig = soft(-label * logits(unit[IMAGE], unit[TEXT]))
    loss_acc[...] = narrowed(plus)
    coef = (-label * sig * sharp).astype(jnp.bfloat16)
    image_acc[...] = jnp.dot(coef, unit[TEXT], preferred_element_type=jnp.float32)
    text_acc[...] = lax.dot_general(
        coef, unit[IMAGE], (((0,), (0,)), ((), ())), preferred_element_type=jnp.float32
    )

    def score(at):
        texts, images = block[TEXT, at], block[IMAGE, at]
        plus, sig = soft(logits(unit[IMAGE], texts))
        back = 1.0 / (1.0 + jnp.exp(-logits(unit[TEXT], images)))
        loss_acc[...] += narrowed(plus)
        image_acc[...] += jnp.dot(
            (sig * sharp).astype(jnp.bfloat16), texts, preferred_element_type=jnp.float32
        )
        text_acc[...] += jnp.dot(
            (back * sharp).astype(jnp.bfloat16), images, preferred_element_type=jnp.float32
        )

    def await_round(k):
        for side in (TEXT, IMAGE):
            for d in range(1, NX):
                x_copy(side, d, k, False).wait_recv()

    @pl.loop(0, CHUNKS)
    def _(k):
        for side in (IMAGE, TEXT):
            z_copy(side, k).wait_recv()
            for d in X_ORDER:

                @pl.when(x + d >= NX if side == TEXT else x + d < NX)
                def _():
                    x_copy(side, d, k, True).start()

            @pl.when(k + who["window"] < CHUNKS)
            def _():
                z_copy(side, k + who["window"]).start()

            @pl.when(k + who["lead"][side] < CHUNKS)
            def _():
                g_copy(side, k + who["lead"][side]).start()

        @pl.when(k > 0)
        def _():
            await_round(k - 1)
            score(pl.ds((k - 1) * per, per))

    for k in range(CHUNKS // 2):
        for side in (TEXT, IMAGE):
            g_copy(side, k).wait_recv()
    score(slice(g_at + half, g_at + rows))
    await_round(CHUNKS - 1)
    for k in range(CHUNKS // 2, CHUNKS):
        for side in (TEXT, IMAGE):
            g_copy(side, k).wait_recv()
    score(slice(g_at - per, g_at + half))

    loss_out[...] = jnp.sum(loss_acc[...].T, axis=0, keepdims=True)

    @pl.loop(0, CHUNKS)
    def _(k):
        for side in (IMAGE, TEXT):
            z_copy(side, k).wait_send()
            g_copy(side, k).wait_send()
            for d in range(1, NX):
                x_copy(side, d, k, False).wait_send()


def finish(
    image_acc, text_acc, image_raw, text_raw, loss, loss_out, image_out, text_out, grad, out_sem
):
    rows = image_acc.shape[0]
    loss_out[...] = loss[0]
    pieces = out_sem.shape[1]
    part = rows // pieces
    copies = []
    for side, acc, raw, out in (
        (IMAGE, image_acc, image_raw, image_out),
        (TEXT, text_acc, text_raw, text_out),
    ):
        for p in range(pieces):
            at = pl.ds(p * part, part)
            rawf = raw[at].astype(jnp.float32)
            grads = acc[at]
            scale = 1.0 / jnp.sqrt(jnp.sum(rawf * rawf, axis=-1, keepdims=True) + 1e-06)
            inner = jnp.sum(rawf * grads, axis=-1, keepdims=True)
            grad[side, at] = ((grads - rawf * (inner * scale * scale)) * scale).astype(grad.dtype)
            copies.append(
                pltpu.make_async_copy(grad.at[side, at], out.at[at], out_sem.at[side, p])
            )
            copies[-1].start()
    for copy in copies:
        copy.wait()


def on_device(picture_embeds_raw, caption_embeds_raw, sharpness_factor, additive_shift_term):
    rows, width = picture_embeds_raw.shape
    part = rows // CHUNKS
    kind = picture_embeds_raw.dtype
    vmem, any_ = pl.BlockSpec(memory_space=pltpu.VMEM), pl.BlockSpec(memory_space=pl.ANY)
    hbm = pl.BlockSpec(memory_space=pltpu.HBM)
    dma = pltpu.SemaphoreType.DMA
    smem = pl.BlockSpec(memory_space=pltpu.SMEM)
    sums = pl.pallas_call(
        exchange,
        out_shape=(
            pltpu.VMEM((rows, width), jnp.float32),
            pltpu.VMEM((rows, width), jnp.float32),
            pltpu.VMEM((rows, width), kind),
            pltpu.VMEM((rows, width), kind),
            pltpu.VMEM((1, rows), jnp.float32),
        ),
        in_specs=[smem, smem, hbm, hbm],
        out_specs=(vmem,) * 5,
        scratch_shapes=[
            pltpu.VMEM((2, rows, width), jnp.bfloat16),
            pltpu.VMEM((2, (NX + 1) * rows, width), jnp.bfloat16),
            pltpu.VMEM((rows, min(128, NX * part)), jnp.float32),
            dma((2, 2)),
            dma((2, CHUNKS)),
            dma((2, CHUNKS)),
            dma((2, NX - 1, CHUNKS)),
            dma((2, NX - 1, CHUNKS)),
            dma((2, CHUNKS)),
            dma((2, CHUNKS)),
        ],
        compiler_params=pltpu.CompilerParams(
            collective_id=0, has_side_effects=True, vmem_limit_bytes=28 << 20
        ),
        name="exchange",
    )(
        sharpness_factor.reshape(1, 1),
        additive_shift_term.reshape(1, 1),
        pltpu.with_memory_space_constraint(picture_embeds_raw, pltpu.HBM),
        pltpu.with_memory_space_constraint(caption_embeds_raw, pltpu.HBM),
    )
    return pl.pallas_call(
        finish,
        out_shape=(
            jax.ShapeDtypeStruct((rows,), jnp.float32),
            jax.ShapeDtypeStruct((rows, width), kind),
            jax.ShapeDtypeStruct((rows, width), kind),
        ),
        in_specs=[vmem] * 5,
        out_specs=(vmem, any_, any_),
        scratch_shapes=[pltpu.VMEM((2, rows, width), kind), dma((2, 2))],
        compiler_params=pltpu.CompilerParams(vmem_limit_bytes=16 << 20),
        name="finish",
    )(*sums)


def solution(mesh):
    in_specs = (P(("blk", "group"), None), P(("blk", "group"), None), P(), P())
    out_specs = (P(("blk", "group")), P(("blk", "group"), None), P(("blk", "group"), None))
    return jax.shard_map(
        on_device, mesh=mesh, in_specs=in_specs, out_specs=out_specs, check_vma=False
    )
```

```python
import functools
import jax
import jax.numpy as jnp
from jax import lax
from jax.experimental import pallas as pl
from jax.experimental.pallas import tpu as pltpu
from jax.sharding import PartitionSpec as P

MESH = pl.DeviceIdType.MESH
NX = 4
CHUNKS = 8
RUN = 4
G_LEAD = 1
X_ORDER = (2, 1, 3)
IMAGE, TEXT = 0, 1


def partners():
    blk, group = lax.axis_index("blk"), lax.axis_index("group")
    n_blk, n_group = lax.axis_size("blk"), lax.axis_size("group")
    x = lax.rem(blk, NX)
    plane = blk - x
    lane = lax.rem(group // 2, RUN)
    core = lax.rem(group, 2)
    wraps = (core == 1) & (lane == RUN - 1)
    return dict(
        x=x,
        window=jnp.where(lane == 0, CHUNKS, jnp.where(wraps, 6, 4)),
        lead={
            TEXT: jnp.where(wraps, CHUNKS, G_LEAD),
            IMAGE: G_LEAD,
        },
        ahead=(lax.rem(blk + NX, n_blk), group),
        behind=(lax.rem(blk + n_blk - NX, n_blk), group),
        along=[None] + [(plane + lax.rem(x + d, NX), group) for d in range(1, NX)],
        after=(blk, lax.rem(group + 1, n_group)),
        before=(blk, lax.rem(group + n_group - 1, n_group)),
    )


def exchange(
    sharp_ref, shift_ref, pic, cap,
    image_acc, text_acc, image_raw, text_raw, loss_out,
    unit, block, loss_acc,
    in_sem, z_send, z_recv, x_send, x_recv, g_send, g_recv,
):
    rows, width = unit.shape[1], unit.shape[2]
    part = rows // CHUNKS
    half = rows // 2
    per = NX * part
    g_at = CHUNKS * per
    sharp, shift = sharp_ref[0, 0], shift_ref[0, 0]
    who = partners()
    x = who["x"]

    pieces = ((0, 1), (1, CHUNKS // 2), (CHUNKS // 2, CHUNKS))

    def rows_of(h):
        return pl.ds(pieces[h][0] * part, (pieces[h][1] - pieces[h][0]) * part)

    def load(h, side, src, dst):
        at = rows_of(h)
        return pltpu.make_async_copy(src.at[at], dst.at[at], in_sem.at[side, h])

    inputs = ((IMAGE, pic, image_raw), (TEXT, cap, text_raw))
    for h in range(len(pieces)):
        for which in inputs:
            load(h, *which).start()

    barrier = pltpu.get_barrier_semaphore()
    others = [who["ahead"], who["behind"], who["after"], who["before"]] + who["along"][1:]
    for other in others:
        pl.semaphore_signal(barrier, inc=1, device_id=other, device_id_type=MESH)

    def z_copy(side, k):
        return pltpu.make_async_remote_copy(
            src_ref=unit.at[side, pl.ds(k * part, part)],
            dst_ref=block.at[side, pl.ds(k * per, part)],
            send_sem=z_send.at[side, k],
            recv_sem=z_recv.at[side, k],
            device_id=who["ahead"] if side == TEXT else who["behind"],
            device_id_type=MESH,
        )

    def x_copy(side, d, k, late):
        own = unit.at[side, pl.ds(k * part, part)]
        return pltpu.make_async_remote_copy(
            src_ref=block.at[side, pl.ds(k * per, part)] if late else own,
            dst_ref=block.at[side, pl.ds(k * per + d * part, part)],
            send_sem=x_send.at[side, d - 1, k],
            recv_sem=x_recv.at[side, d - 1, k],
            device_id=who["along"][d],
            device_id_type=MESH,
        )

    def g_copy(side, k):
        to = lax.rem(k * part + half, rows)
        return pltpu.make_async_remote_copy(
            src_ref=unit.at[side, pl.ds(k * part, part)],
            dst_ref=block.at[side, pl.ds(g_at + to, part)],
            send_sem=g_send.at[side, k],
            recv_sem=g_recv.at[side, k],
            device_id=who["after"] if side == TEXT else who["before"],
            device_id_type=MESH,
        )

    def normalize(h):
        at = rows_of(h)
        for side, src, raw in inputs:
            load(h, side, src, raw).wait()
            rawf = raw[at].astype(jnp.float32)
            scale = 1.0 / jnp.sqrt(jnp.sum(rawf * rawf, axis=-1, keepdims=True) + 1e-06)
            unit[side, at] = (rawf * scale).astype(jnp.bfloat16)

    normalize(0)
    pl.semaphore_wait(barrier, len(others))
    for h, piece in enumerate(pieces):
        if h > 0:
            normalize(h)
        for k in range(*piece):
            for side in (IMAGE, TEXT):

                @pl.when(k < who["window"])
                def _():
                    z_copy(side, k).start()

                @pl.when(k < who["lead"][side])
                def _():
                    g_copy(side, k).start()

    @pl.loop(0, CHUNKS)
    def _(k):
        for d in X_ORDER:

            @pl.when(x + d < NX)
            def _():
                x_copy(TEXT, d, k, False).start()

            @pl.when(x + d >= NX)
            def _():
                x_copy(IMAGE, d, k, False).start()

    def logits(mine, theirs):
        dots = lax.dot_general(
            mine, theirs, (((1,), (1,)), ((), ())), preferred_element_type=jnp.float32
        )
        return dots * sharp + shift

    def soft(v):
        small = jnp.exp(-jnp.abs(v))
        plus = jnp.maximum(v, 0.0) + jnp.log1p(small)
        return plus, jnp.where(v >= 0.0, 1.0, small) / (1.0 + small)

    lanes = loss_acc.shape[1]

    def narrowed(plus):
        return sum(plus[:, i : i + lanes] for i in range(0, plus.shape[1], lanes))

    same = lax.broadcasted_iota(jnp.int32, (rows, rows), 0) == lax.broadcasted_iota(
        jnp.int32, (rows, rows), 1
    )
    label = jnp.where(same, 1.0, -1.0)
    plus, sig = soft(-label * logits(unit[IMAGE], unit[TEXT]))
    loss_acc[...] = narrowed(plus)
    coef = (-label * sig * sharp).astype(jnp.bfloat16)
    image_acc[...] = jnp.dot(coef, unit[TEXT], preferred_element_type=jnp.float32)
    text_acc[...] = lax.dot_general(
        coef, unit[IMAGE], (((0,), (0,)), ((), ())), preferred_element_type=jnp.float32
    )

    def score(at):
        texts, images = block[TEXT, at], block[IMAGE, at]
        plus, sig = soft(logits(unit[IMAGE], texts))
        back = 1.0 / (1.0 + jnp.exp(-logits(unit[TEXT], images)))
        loss_acc[...] += narrowed(plus)
        image_acc[...] += jnp.dot(
            (sig * sharp).astype(jnp.bfloat16), texts, preferred_element_type=jnp.float32
        )
        text_acc[...] += jnp.dot(
            (back * sharp).astype(jnp.bfloat16), images, preferred_element_type=jnp.float32
        )

    def await_sent(k):
        for side in (IMAGE, TEXT):
            z_copy(side, k).wait_send()
            g_copy(side, k).wait_send()
            for d in range(1, NX):
                x_copy(side, d, k, False).wait_send()

    def await_round(k):
        for side in (TEXT, IMAGE):
            for d in range(1, NX):
                x_copy(side, d, k, False).wait_recv()

    @pl.loop(0, CHUNKS)
    def _(k):
        for side in (IMAGE, TEXT):
            z_copy(side, k).wait_recv()
            for d in X_ORDER:

                @pl.when(x + d >= NX if side == TEXT else x + d < NX)
                def _():
                    x_copy(side, d, k, True).start()

            @pl.when(k + who["window"] < CHUNKS)
            def _():
                z_copy(side, k + who["window"]).start()

            @pl.when(k + who["lead"][side] < CHUNKS)
            def _():
                g_copy(side, k + who["lead"][side]).start()

        @pl.when(k > 0)
        def _():
            await_round(k - 1)
            score(pl.ds((k - 1) * per, per))

    @pl.loop(0, CHUNKS - 2)
    def _(k):
        await_sent(k)

    for k in range(CHUNKS // 2):
        for side in (TEXT, IMAGE):
            g_copy(side, k).wait_recv()
    score(slice(g_at + half, g_at + rows))
    await_round(CHUNKS - 1)
    for k in range(CHUNKS // 2, CHUNKS):
        for side in (TEXT, IMAGE):
            g_copy(side, k).wait_recv()
    score(slice(g_at - per, g_at + half))

    loss_out[...] = jnp.sum(loss_acc[...].T, axis=0, keepdims=True)

    for k in range(CHUNKS - 2, CHUNKS):
        await_sent(k)


def finish(
    image_acc, text_acc, image_raw, text_raw, loss, loss_out, image_out, text_out, grad, out_sem
):
    rows = image_acc.shape[0]
    loss_out[...] = loss[0]
    pieces = out_sem.shape[1]
    part = rows // pieces
    copies = []
    for side, acc, raw, out in (
        (IMAGE, image_acc, image_raw, image_out),
        (TEXT, text_acc, text_raw, text_out),
    ):
        for p in range(pieces):
            at = pl.ds(p * part, part)
            rawf = raw[at].astype(jnp.float32)
            grads = acc[at]
            scale = 1.0 / jnp.sqrt(jnp.sum(rawf * rawf, axis=-1, keepdims=True) + 1e-06)
            inner = jnp.sum(rawf * grads, axis=-1, keepdims=True)
            grad[side, at] = ((grads - rawf * (inner * scale * scale)) * scale).astype(grad.dtype)
            copies.append(
                pltpu.make_async_copy(grad.at[side, at], out.at[at], out_sem.at[side, p])
            )
            copies[-1].start()
    for copy in copies:
        copy.wait()


def on_device(picture_embeds_raw, caption_embeds_raw, sharpness_factor, additive_shift_term):
    rows, width = picture_embeds_raw.shape
    part = rows // CHUNKS
    kind = picture_embeds_raw.dtype
    vmem, any_ = pl.BlockSpec(memory_space=pltpu.VMEM), pl.BlockSpec(memory_space=pl.ANY)
    hbm = pl.BlockSpec(memory_space=pltpu.HBM)
    dma = pltpu.SemaphoreType.DMA
    smem = pl.BlockSpec(memory_space=pltpu.SMEM)
    sums = pl.pallas_call(
        exchange,
        out_shape=(
            pltpu.VMEM((rows, width), jnp.float32),
            pltpu.VMEM((rows, width), jnp.float32),
            pltpu.VMEM((rows, width), kind),
            pltpu.VMEM((rows, width), kind),
            pltpu.VMEM((1, rows), jnp.float32),
        ),
        in_specs=[smem, smem, hbm, hbm],
        out_specs=(vmem,) * 5,
        scratch_shapes=[
            pltpu.VMEM((2, rows, width), jnp.bfloat16),
            pltpu.VMEM((2, (NX + 1) * rows, width), jnp.bfloat16),
            pltpu.VMEM((rows, min(128, NX * part)), jnp.float32),
            dma((2, 3)),
            dma((2, CHUNKS)),
            dma((2, CHUNKS)),
            dma((2, NX - 1, CHUNKS)),
            dma((2, NX - 1, CHUNKS)),
            dma((2, CHUNKS)),
            dma((2, CHUNKS)),
        ],
        compiler_params=pltpu.CompilerParams(
            collective_id=0, has_side_effects=True, vmem_limit_bytes=28 << 20
        ),
        name="exchange",
    )(
        sharpness_factor.reshape(1, 1),
        additive_shift_term.reshape(1, 1),
        pltpu.with_memory_space_constraint(picture_embeds_raw, pltpu.HBM),
        pltpu.with_memory_space_constraint(caption_embeds_raw, pltpu.HBM),
    )
    return pl.pallas_call(
        finish,
        out_shape=(
            jax.ShapeDtypeStruct((rows,), jnp.float32),
            jax.ShapeDtypeStruct((rows, width), kind),
            jax.ShapeDtypeStruct((rows, width), kind),
        ),
        in_specs=[vmem] * 5,
        out_specs=(vmem, any_, any_),
        scratch_shapes=[pltpu.VMEM((2, rows, width), kind), dma((2, 2))],
        compiler_params=pltpu.CompilerParams(vmem_limit_bytes=16 << 20),
        name="finish",
    )(*sums)


def solution(mesh):
    in_specs = (P(("blk", "group"), None), P(("blk", "group"), None), P(), P())
    out_specs = (P(("blk", "group")), P(("blk", "group"), None), P(("blk", "group"), None))
    return jax.shard_map(
        on_device, mesh=mesh, in_specs=in_specs, out_specs=out_specs, check_vma=False
    )
```
